768 devices in a mesh: row: 24 (over z_lo, y), col: 32 (over x, z_hi, core).
Axes of the slice: x: 4, y: 8, z: 12 (z_hi: 4, z_lo: 3; z = z_hi * 3 + z_lo), core: 2. Of those that a mesh axis runs over, the one named last changes fastest.
Arguments:
- amplitudes: bfloat16 [768, 49152], P('row', 'col'), may hold values from -6 to 6
- amp_tiles: int32 [12, 768], P(None, 'col'), may hold values from 0 to 1, as said below
- integrals: bfloat16 [30720, 49152], P('row', 'col'), may hold values from -0.0390625 to 0.0390625
- int_tiles: int32 [480, 768], P('row', 'col'), may hold values from 0 to 1, as said below
- prior: float32 [768, 30720], P('col', 'row'), may hold values from -6 to 6
Outputs:
- ladder: float32 [768, 30720], P('col', 'row')
The draws below stay inside these ranges and needn't reach their ends.
Inputs may be any that keep to these rules, and one draw needn't show every extreme that they name: `amp_tiles`: each entry flags one tile as nonzero (1) or zero (0). `int_tiles`: each entry flags one tile as nonzero (1) or zero (0); some rows of tiles are zero throughout.
All inputs are finite; a program needn't handle non-finite values.
Results may differ from the reference program's by a relative error of at most 0.0003.
Values may be sent and summed in bfloat16 or wider, within the bound.
No kernel may reach another device: no remote copies, remote signals or barrier semaphores. Data moves between devices by JAX's collectives and lax.ppermute only.
A program may use at most 64 MiB of HBM per device.

```python
import jax
import jax.numpy as jnp
from jax import lax

TILE = 64
IJ = 768
AB_TILES_DEV = 20
AB_TILES = 480
CD_TILES = 768
AB = 30720
CD = 49152
N_ROW = 24


def draw_amp_tiles(key, part):
    key = jax.random.fold_in(key, 11)
    level_key, entry_key = jax.random.split(key)
    levels = jax.random.randint(level_key, (IJ // TILE, 1), 1, 5)
    entries = jax.random.randint(entry_key, (IJ // TILE, CD_TILES), 0, 4)
    return jnp.where(entries < levels, 1, 0).astype(jnp.int32)


def draw_int_tiles(key, part):
    key = jax.random.fold_in(key, 23)
    level_key, entry_key = jax.random.split(key)
    levels = jax.random.randint(level_key, (AB_TILES, 1), 0, 5)
    entries = jax.random.randint(entry_key, (AB_TILES, CD_TILES), 0, 4)
    return jnp.where(entries < levels, 1, 0).astype(jnp.int32)


def strengthened(values, stream_key, source, target, shards_of, factor):
    owner, partner = [(jnp.arange(values.shape[axis_at]) // (values.shape[axis_at] // shards_of)).reshape([-1 if axis == axis_at else 1 for axis in range(values.ndim)]) for axis_at in (source, target)]
    chosen = jax.random.permutation(stream_key, shards_of)[partner]
    strong = (owner == chosen) | (owner == (partner + shards_of // 2) % shards_of)
    return jnp.where(strong, factor * values, values)


def block_levels(key, extent, cuts, low, top_value):
    def one(axis_at, shards_of):
        steps = jax.random.uniform(jax.random.fold_in(jax.random.fold_in(key, 6), axis_at), (shards_of,), jnp.float32, low / len(cuts), top_value / len(cuts))
        return jnp.repeat(jnp.exp(steps), extent[axis_at] // shards_of).reshape((-1,) + (1,) * (len(extent) - axis_at - 1))

    gain = one(*cuts[0])
    for cut in cuts[1:]:
        gain = gain * one(*cut)
    return gain


def normal_values(stream_key, extent, spread, bound, shards=(), dtype=jnp.bfloat16):
    level = block_levels(stream_key, extent, shards, -0.22, 0.18) if shards else 1.0
    values = jax.random.normal(stream_key, extent, jnp.float32) * spread * level
    return jnp.minimum(jnp.maximum(values, -bound), bound).astype(dtype)


def gaussian_with(stream_key, shape, scale, limit, pieces, heavy, dtype=jnp.bfloat16):
    values = scale * jax.random.normal(stream_key, shape, jnp.float32)
    if pieces:
        values = values * block_levels(stream_key, shape, pieces, -0.22, 0.18)
    return jnp.clip(strengthened(values, jax.random.fold_in(stream_key, 3), *heavy), -limit, limit).astype(dtype)


def setup_inputs(seed: int = 0) -> dict:
    streams_of = jax.random.split(jax.random.key(seed), 6)
    return {
        "amplitudes": gaussian_with(streams_of[0], (IJ, CD), 1.0, 6.0, ((0, 24), (1, 32)), (1, 0, 32, 2.75)),
        "amp_tiles": draw_amp_tiles(jax.random.fold_in(streams_of[5], 71), 0),
        "integrals": normal_values(streams_of[2], (AB, CD), (CD // 2) ** -0.5, 0.0390625, ((0, 24), (1, 32))),
        "int_tiles": draw_int_tiles(jax.random.fold_in(streams_of[5], 71), 0),
        "prior": normal_values(streams_of[4], (IJ, AB), 1.0, 6.0, ((0, 32), (1, 24)), jnp.float32),
    }


def reference(amplitudes, amp_tiles, integrals, int_tiles, prior):
    masked_amps = (amplitudes.reshape(IJ // TILE, TILE, CD_TILES, TILE) * amp_tiles[:, None, :, None].astype(jnp.bfloat16)).reshape(IJ, CD)
    slabs = integrals.reshape(N_ROW, AB_TILES_DEV, TILE, CD_TILES, TILE)
    slab_masks = int_tiles.reshape(N_ROW, AB_TILES_DEV, CD_TILES)

    def contract_slab(slab_pair):
        slab, slab_mask = slab_pair
        masked = (slab * slab_mask[:, None, :, None].astype(jnp.bfloat16)).reshape(AB_TILES_DEV * TILE, CD)
        return lax.dot_general(masked_amps, masked, (((1,), (1,)), ((), ())), preferred_element_type=jnp.float32)

    blocks = lax.map(contract_slab, (slabs, slab_masks))
    ladder_term = blocks.transpose(1, 0, 2).reshape(IJ, AB)
    return prior + ladder_term
```

```python
import jax
import jax.numpy as jnp
from jax import lax
from jax.experimental import pallas as pl
from jax.experimental.pallas import tpu as pltpu
from jax.sharding import Mesh, PartitionSpec as P

AXES = ("zlo", "y", "x", "zhi", "core")
SIZES = (3, 8, 4, 4, 2)
ROW = ("zlo", "y")
COL = ("x", "zhi", "core")
TILE = 64
BLOCK = 256

AMP_SCALE = 2.0**13
X_SCALE = 2.0**6
Z_SCALE = 2.0**4


def product_kernel(amps_ref, tiles_ref, ints_ref, out_ref, mask_ref):
    @pl.when(pl.program_id(0) == 0)
    def _():
        count, width = tiles_ref.shape[1], ints_ref.shape[1]
        tile_of = lax.shift_right_logical(
            lax.broadcasted_iota(jnp.int32, (count, width), 1), TILE.bit_length() - 1
        )
        spread = (tile_of == lax.broadcasted_iota(jnp.int32, (count, width), 0)).astype(jnp.bfloat16)
        mask_ref[...] = jnp.dot(
            tiles_ref[...].astype(jnp.bfloat16), spread, preferred_element_type=jnp.float32
        )

    first = pl.program_id(0) * (BLOCK // TILE)
    parts = []
    for k in range(BLOCK // TILE):
        row = mask_ref[pl.ds(first + k, 1), :].astype(jnp.bfloat16)
        parts.append(ints_ref[k * TILE : (k + 1) * TILE, :] * row)
    masked = jnp.concatenate(parts, axis=0)
    out_ref[...] = lax.dot_general(
        amps_ref[...], masked, (((1,), (1,)), ((), ())), preferred_element_type=jnp.float32
    )


def product(amps, int_tiles, integrals):
    rows, depth = amps.shape
    ab = integrals.shape[0]
    return pl.pallas_call(
        product_kernel,
        grid=(ab // BLOCK,),
        in_specs=[
            pl.BlockSpec((rows, depth), lambda b: (0, 0)),
            pl.BlockSpec(int_tiles.shape, lambda b: (0, 0)),
            pl.BlockSpec((BLOCK, depth), lambda b: (b, 0)),
        ],
        out_specs=pl.BlockSpec((rows, BLOCK), lambda b: (0, b)),
        out_shape=jax.ShapeDtypeStruct((rows, ab), jnp.float32),
        scratch_shapes=[pltpu.VMEM((int_tiles.shape[0], depth), jnp.float32)],
        compiler_params=pltpu.CompilerParams(vmem_limit_bytes=40 * 2**20),
        cost_estimate=pl.CostEstimate(
            flops=2 * rows * ab * depth, bytes_accessed=2 * (rows + ab) * depth + 4 * rows * ab, transcendentals=0
        ),
    )(amps, int_tiles, integrals)


def on_device(amplitudes, amp_tiles, integrals, int_tiles, prior):
    f16, f32 = jnp.float16, jnp.float32
    local_rows, depth = amplitudes.shape
    ab = integrals.shape[0]
    own_rows = prior.shape[0]
    core, x, zhi = lax.axis_index("core"), lax.axis_index("x"), lax.axis_index("zhi")
    row = lax.axis_index(ROW)
    n_x, n_zhi, n_core = lax.axis_size("x"), lax.axis_size("zhi"), lax.axis_size("core")

    flags = lax.dynamic_slice_in_dim(amp_tiles, row * local_rows // TILE, 1, 0)
    mask = jnp.repeat(flags.astype(f32) * AMP_SCALE, TILE, axis=1)
    sent = (amplitudes.astype(f32) * mask).astype(f16)
    near = lax.all_gather(sent, "zlo", axis=0, tiled=False)
    amps = lax.all_gather(near, "y", axis=1, tiled=False)
    amps = amps.astype(jnp.bfloat16).reshape(n_x, n_zhi, n_core, own_rows, depth)
    amps = amps.transpose(2, 0, 1, 3, 4).reshape(n_core, n_x * n_zhi * own_rows, depth)

    other = product(lax.dynamic_index_in_dim(amps, 1 - core, 0, False), int_tiles, integrals)
    crossing = lax.ppermute(other, "core", [(0, 1), (1, 0)])
    mine = product(lax.dynamic_index_in_dim(amps, core, 0, False), int_tiles, integrals)
    total = ((mine + crossing) * (X_SCALE / AMP_SCALE)).reshape(n_x, n_zhi * own_rows, ab)

    got = lax.all_to_all(total.astype(f16), "x", 0, 0, tiled=True)
    total = got.astype(f32).sum(0) * (Z_SCALE / X_SCALE)
    total = total.reshape(n_zhi, own_rows, ab)
    got = lax.all_to_all(total.astype(f16), "zhi", 0, 0, tiled=True)
    return prior + got.astype(f32).sum(0) * (1 / Z_SCALE)


def solution(mesh):
    parts = Mesh(mesh.devices.reshape(SIZES), AXES)
    in_specs = (P(ROW, COL), P(None, COL), P(ROW, COL), P(ROW, COL), P(COL, ROW))
    return jax.shard_map(
        on_device, mesh=parts, in_specs=in_specs, out_specs=P(COL, ROW), check_vma=False
    )
```

```python
import jax
import jax.numpy as jnp
from jax import lax
from jax.experimental import pallas as pl
from jax.experimental.pallas import tpu as pltpu
from jax.sharding import Mesh, PartitionSpec as P

AXES = ("zlo", "y", "x", "zhi", "core")
SIZES = (3, 8, 4, 4, 2)
ROW = ("zlo", "y")
COL = ("x", "zhi", "core")
TILE = 64
BLOCK = 256
PIECE = 128
VMEM_LIMIT = 24 * 2**20

AMP_SCALE = 2.0**13
X_SCALE = 2.0**6
Z_SCALE = 2.0**4


def dot(a, b):
    return lax.dot_general(a, b, (((1,), (1,)), ((), ())), preferred_element_type=jnp.float32)


def spread_flags(flags, width):
    count = flags.shape[1]
    tile_of = lax.shift_right_logical(
        lax.broadcasted_iota(jnp.int32, (count, width), 1), TILE.bit_length() - 1
    )
    spread = (tile_of == lax.broadcasted_iota(jnp.int32, (count, width), 0)).astype(jnp.bfloat16)
    return jnp.dot(flags.astype(jnp.bfloat16), spread, preferred_element_type=jnp.float32)


def masks_kernel(first_ref, amp_tiles_ref, int_tiles_ref, ints_ref, amp_mask_ref, masked_ref, spread_ref, flags_ref, sems):
    depth = amp_mask_ref.shape[1]
    pieces = [pl.ds(start, PIECE) for start in range(0, masked_ref.shape[0], PIECE)]
    flags_copy = pltpu.make_async_copy(int_tiles_ref, flags_ref, sems.at[len(pieces)])
    flags_copy.start()
    copies = [
        pltpu.make_async_copy(ints_ref.at[piece, :], masked_ref.at[piece, :], sems.at[at])
        for at, piece in enumerate(pieces)
    ]
    for copy in copies:
        copy.start()
    spread_ref[...] = spread_flags(amp_tiles_ref[...], depth) * AMP_SCALE
    parts = amp_mask_ref.shape[0]
    step = amp_tiles_ref.shape[0] // parts
    for part in range(parts):
        amp_mask_ref[part : part + 1, :] = spread_ref[pl.ds(part * step + first_ref[0], 1), :]
    flags_copy.wait()
    int_mask = spread_flags(flags_ref[...], depth).astype(jnp.bfloat16)
    for at, copy in enumerate(copies):
        copy.wait()
        for start in range(at * PIECE, (at + 1) * PIECE, TILE):
            rows = slice(start, start + TILE)
            tile = start // TILE
            masked_ref[rows, :] = masked_ref[rows, :] * int_mask[tile : tile + 1, :]


def masks(first, parts, amp_tiles, int_tiles, integrals):
    ab, depth = integrals.shape
    vmem, hbm = pl.BlockSpec(memory_space=pltpu.VMEM), pl.BlockSpec(memory_space=pltpu.HBM)
    return pl.pallas_call(
        masks_kernel,
        in_specs=[pl.BlockSpec(memory_space=pltpu.SMEM), vmem, hbm, hbm],
        out_specs=[vmem, vmem],
        out_shape=[
            jax.ShapeDtypeStruct((parts, depth), jnp.float32),
            jax.ShapeDtypeStruct((ab, depth), jnp.bfloat16),
        ],
        scratch_shapes=[
            pltpu.VMEM((amp_tiles.shape[0], depth), jnp.float32),
            pltpu.VMEM(int_tiles.shape, jnp.int32),
            pltpu.SemaphoreType.DMA((ab // PIECE + 1,)),
        ],
        compiler_params=pltpu.CompilerParams(vmem_limit_bytes=VMEM_LIMIT),
        cost_estimate=pl.CostEstimate(flops=ab * depth, bytes_accessed=4 * ab * depth, transcendentals=0),
    )(
        jnp.full((1,), first, jnp.int32),
        amp_tiles,
        pltpu.with_memory_space_constraint(int_tiles, pltpu.HBM),
        pltpu.with_memory_space_constraint(integrals, pltpu.HBM),
    )


def product_kernel(amps_ref, masked_ref, out_ref):
    for start in range(0, masked_ref.shape[0], BLOCK):
        block = slice(start, start + BLOCK)
        out_ref[:, block] = dot(amps_ref[...], masked_ref[block, :])


def product(amps, masked):
    rows, depth = amps.shape
    ab = masked.shape[0]
    vmem = pl.BlockSpec(memory_space=pltpu.VMEM)
    return pl.pallas_call(
        product_kernel,
        in_specs=[vmem, vmem],
        out_specs=vmem,
        out_shape=jax.ShapeDtypeStruct((rows, ab), jnp.float32),
        compiler_params=pltpu.CompilerParams(vmem_limit_bytes=VMEM_LIMIT),
        cost_estimate=pl.CostEstimate(
            flops=2 * rows * ab * depth, bytes_accessed=2 * (rows + ab) * depth + 4 * rows * ab, transcendentals=0
        ),
    )(amps, masked)


def sum_scatter(values, axis):
    sent = values.astype(jnp.float16)
    got = lax.all_to_all(sent, axis, 0, 0, tiled=True).astype(jnp.float32)
    return got.sum(0)


def on_device(amplitudes, amp_tiles, integrals, int_tiles, prior):
    f16, f32 = jnp.float16, jnp.float32
    local_rows, depth = amplitudes.shape
    ab = integrals.shape[0]
    own_rows = prior.shape[0]
    core, y = lax.axis_index("core"), lax.axis_index("y")
    n_x, n_zhi, n_core = lax.axis_size("x"), lax.axis_size("zhi"), lax.axis_size("core")

    zlo, n_zlo = lax.axis_index("zlo"), lax.axis_size("zlo")
    mask, masked = masks(y * local_rows // TILE, n_zlo, amp_tiles, int_tiles, integrals)
    held = [amplitudes]
    for hop in range(1, n_zlo):
        held.append(lax.ppermute(amplitudes, "zlo", [(i, (i + hop) % n_zlo) for i in range(n_zlo)]))
    near = []
    for source in range(n_zlo):
        block = held[0]
        for hop in range(1, n_zlo):
            block = jnp.where((zlo - hop) % n_zlo == source, held[hop], block)
        near.append(block)
    near = jnp.stack(near)
    near = (near.astype(f32) * mask[:, None, :]).astype(f16)
    amps = lax.all_gather(near, "y", axis=1, tiled=False)
    amps = amps.astype(jnp.bfloat16).reshape(n_x, n_zhi, n_core, own_rows, depth)
    amps = amps.transpose(2, 0, 1, 3, 4).reshape(n_core, n_x * n_zhi * own_rows, depth)

    other = product(lax.dynamic_index_in_dim(amps, 1 - core, 0, False), masked)
    crossing = lax.ppermute(other, "core", [(0, 1), (1, 0)])
    mine = product(lax.dynamic_index_in_dim(amps, core, 0, False), masked)
    total = (mine + crossing) * (X_SCALE / AMP_SCALE)
    total = sum_scatter(total.reshape(n_x, n_zhi * own_rows, ab), "x") * (Z_SCALE / X_SCALE)
    total = sum_scatter(total.reshape(n_zhi, own_rows, ab), "zhi")
    return prior + total * (1 / Z_SCALE)


def solution(mesh):
    parts = Mesh(mesh.devices.reshape(SIZES), AXES)
    in_specs = (P(ROW, COL), P(None, COL), P(ROW, COL), P(ROW, COL), P(COL, ROW))
    return jax.shard_map(
        on_device, mesh=parts, in_specs=in_specs, out_specs=P(COL, ROW), check_vma=False
    )
```

```python
import jax
import jax.numpy as jnp
from jax import lax
from jax.experimental import pallas as pl
from jax.experimental.pallas import tpu as pltpu
from jax.sharding import Mesh, PartitionSpec as P

AXES = ("zlo", "y", "x", "zhi", "core")
SIZES = (3, 8, 4, 4, 2)
ROW = ("zlo", "y")
COL = ("x", "zhi", "core")
TILE = 64
BLOCK = 256
PIECE = 128
VMEM_LIMIT = 24 * 2**20

AMP_SCALE = 2.0**13
X_SCALE = 2.0**6
Z_SCALE = 2.0**4


def dot(a, b):
    return lax.dot_general(a, b, (((1,), (1,)), ((), ())), preferred_element_type=jnp.float32)


def spread_flags(flags, width):
    count = flags.shape[1]
    tile_of = lax.shift_right_logical(
        lax.broadcasted_iota(jnp.int32, (count, width), 1), TILE.bit_length() - 1
    )
    spread = (tile_of == lax.broadcasted_iota(jnp.int32, (count, width), 0)).astype(jnp.bfloat16)
    return jnp.dot(flags.astype(jnp.bfloat16), spread, preferred_element_type=jnp.float32)


def masks_kernel(first_ref, amp_tiles_ref, int_tiles_ref, ints_ref, amp_mask_ref, masked_ref, spread_ref, flags_ref, sems):
    depth = amp_mask_ref.shape[1]
    pieces = [pl.ds(start, PIECE) for start in range(0, masked_ref.shape[0], PIECE)]
    flags_copy = pltpu.make_async_copy(int_tiles_ref, flags_ref, sems.at[len(pieces)])
    flags_copy.start()
    copies = [
        pltpu.make_async_copy(ints_ref.at[piece, :], masked_ref.at[piece, :], sems.at[at])
        for at, piece in enumerate(pieces)
    ]
    for copy in copies:
        copy.start()
    spread_ref[...] = spread_flags(amp_tiles_ref[...], depth) * AMP_SCALE
    parts = amp_mask_ref.shape[0]
    step = amp_tiles_ref.shape[0] // parts
    for part in range(parts):
        amp_mask_ref[part : part + 1, :] = spread_ref[pl.ds(part * step + first_ref[0], 1), :]
    flags_copy.wait()
    int_mask = spread_flags(flags_ref[...], depth).astype(jnp.bfloat16)
    for at, copy in enumerate(copies):
        copy.wait()
        for start in range(at * PIECE, (at + 1) * PIECE, TILE):
            rows = slice(start, start + TILE)
            tile = start // TILE
            masked_ref[rows, :] = masked_ref[rows, :] * int_mask[tile : tile + 1, :]


def masks(first, parts, amp_tiles, int_tiles, integrals):
    ab, depth = integrals.shape
    vmem, hbm = pl.BlockSpec(memory_space=pltpu.VMEM), pl.BlockSpec(memory_space=pltpu.HBM)
    return pl.pallas_call(
        masks_kernel,
        in_specs=[pl.BlockSpec(memory_space=pltpu.SMEM), vmem, hbm, hbm],
        out_specs=[vmem, vmem],
        out_shape=[
            jax.ShapeDtypeStruct((parts, depth), jnp.float32),
            jax.ShapeDtypeStruct((ab, depth), jnp.bfloat16),
        ],
        scratch_shapes=[
            pltpu.VMEM((amp_tiles.shape[0], depth), jnp.float32),
            pltpu.VMEM(int_tiles.shape, jnp.int32),
            pltpu.SemaphoreType.DMA((ab // PIECE + 1,)),
        ],
        compiler_params=pltpu.CompilerParams(vmem_limit_bytes=VMEM_LIMIT),
        cost_estimate=pl.CostEstimate(flops=ab * depth, bytes_accessed=4 * ab * depth, transcendentals=0),
    )(
        jnp.full((1,), first, jnp.int32),
        amp_tiles,
        pltpu.with_memory_space_constraint(int_tiles, pltpu.HBM),
        pltpu.with_memory_space_constraint(integrals, pltpu.HBM),
    )


def product_kernel(amps_ref, masked_ref, out_ref):
    for start in range(0, masked_ref.shape[0], BLOCK):
        block = slice(start, start + BLOCK)
        out_ref[:, block] = dot(amps_ref[...], masked_ref[block, :])


def product(amps, masked):
    rows, depth = amps.shape
    ab = masked.shape[0]
    vmem = pl.BlockSpec(memory_space=pltpu.VMEM)
    return pl.pallas_call(
        product_kernel,
        in_specs=[vmem, vmem],
        out_specs=vmem,
        out_shape=jax.ShapeDtypeStruct((rows, ab), jnp.float32),
        compiler_params=pltpu.CompilerParams(vmem_limit_bytes=VMEM_LIMIT),
        cost_estimate=pl.CostEstimate(
            flops=2 * rows * ab * depth, bytes_accessed=2 * (rows + ab) * depth + 4 * rows * ab, transcendentals=0
        ),
    )(amps, masked)


def sum_scatter(values, axis):
    sent = values.astype(jnp.float16)
    got = lax.all_to_all(sent, axis, 0, 0, tiled=True).astype(jnp.float32)
    return got.sum(0)


def on_device(amplitudes, amp_tiles, integrals, int_tiles, prior):
    f16, f32 = jnp.float16, jnp.float32
    local_rows, depth = amplitudes.shape
    ab = integrals.shape[0]
    own_rows = prior.shape[0]
    core, y = lax.axis_index("core"), lax.axis_index("y")
    n_x, n_zhi, n_core = lax.axis_size("x"), lax.axis_size("zhi"), lax.axis_size("core")

    zlo, n_zlo = lax.axis_index("zlo"), lax.axis_size("zlo")
    mask, masked = masks(y * local_rows // TILE, n_zlo, amp_tiles, int_tiles, integrals)
    held = [amplitudes]
    for hop in range(1, n_zlo):
        held.append(lax.ppermute(amplitudes, "zlo", [(i, (i + hop) % n_zlo) for i in range(n_zlo)]))
    near = []
    for source in range(n_zlo):
        block = held[0]
        for hop in range(1, n_zlo):
            block = jnp.where((zlo - hop) % n_zlo == source, held[hop], block)
        near.append(block)
    near = jnp.stack(near)
    near = (near.astype(f32) * mask[:, None, :]).astype(f16)
    amps = lax.all_gather(near, "y", axis=1, tiled=False)
    amps = amps.reshape(n_x, n_zhi, n_core, own_rows, depth)

    def product_of(c):
        rows = lax.dynamic_index_in_dim(amps, c, 2, False).astype(jnp.bfloat16)
        return product(rows.reshape(n_x * n_zhi * own_rows, depth), masked)

    crossing = lax.ppermute(product_of(1 - core), "core", [(0, 1), (1, 0)])
    mine = product_of(core)
    total = (mine + crossing) * (X_SCALE / AMP_SCALE)
    total = sum_scatter(total.reshape(n_x, n_zhi * own_rows, ab), "x") * (Z_SCALE / X_SCALE)
    total = sum_scatter(total.reshape(n_zhi, own_rows, ab), "zhi")
    return prior + total * (1 / Z_SCALE)


def solution(mesh):
    parts = Mesh(mesh.devices.reshape(SIZES), AXES)
    in_specs = (P(ROW, COL), P(None, COL), P(ROW, COL), P(ROW, COL), P(COL, ROW))
    return jax.shard_map(
        on_device, mesh=parts, in_specs=in_specs, out_specs=P(COL, ROW), check_vma=False
    )
```

```python
import jax
import jax.numpy as jnp
from jax import lax
from jax.experimental import pallas as pl
from jax.experimental.pallas import tpu as pltpu
from jax.sharding import Mesh, PartitionSpec as P

AXES = ("zlo", "y", "x", "zhi", "core")
SIZES = (3, 8, 4, 4, 2)
ROW = ("zlo", "y")
COL = ("x", "zhi", "core")
TILE = 64
BLOCK = 256
PIECE = 128
VMEM_LIMIT = 24 * 2**20

AMP_SCALE = 2.0**13
X_SCALE = 2.0**6
Z_SCALE = 2.0**4


def dot(a, b):
    return lax.dot_general(a, b, (((1,), (1,)), ((), ())), preferred_element_type=jnp.float32)


def spread_flags(flags, width):
    count = flags.shape[1]
    tile_of = lax.shift_right_logical(
        lax.broadcasted_iota(jnp.int32, (count, width), 1), TILE.bit_length() - 1
    )
    spread = (tile_of == lax.broadcasted_iota(jnp.int32, (count, width), 0)).astype(jnp.bfloat16)
    return jnp.dot(flags.astype(jnp.bfloat16), spread, preferred_element_type=jnp.float32)


def masks_kernel(first_ref, amp_tiles_ref, int_tiles_ref, ints_ref, amp_mask_ref, masked_ref, spread_ref, flags_ref, sems):
    depth = amp_mask_ref.shape[1]
    pieces = [pl.ds(start, PIECE) for start in range(0, masked_ref.shape[0], PIECE)]
    flags_copy = pltpu.make_async_copy(int_tiles_ref, flags_ref, sems.at[len(pieces)])
    flags_copy.start()
    copies = [
        pltpu.make_async_copy(ints_ref.at[piece, :], masked_ref.at[piece, :], sems.at[at])
        for at, piece in enumerate(pieces)
    ]
    for copy in copies:
        copy.start()
    spread_ref[...] = spread_flags(amp_tiles_ref[...], depth) * AMP_SCALE
    parts = amp_mask_ref.shape[0]
    step = amp_tiles_ref.shape[0] // parts
    for part in range(parts):
        amp_mask_ref[part : part + 1, :] = spread_ref[pl.ds(part * step + first_ref[0], 1), :]
    flags_copy.wait()
    int_mask = spread_flags(flags_ref[...], depth).astype(jnp.bfloat16)
    for at, copy in enumerate(copies):
        copy.wait()
        for start in range(at * PIECE, (at + 1) * PIECE, TILE):
            rows = slice(start, start + TILE)
            tile = start // TILE
            masked_ref[rows, :] = masked_ref[rows, :] * int_mask[tile : tile + 1, :]


def masks(first, parts, amp_tiles, int_tiles, integrals):
    ab, depth = integrals.shape
    vmem, hbm = pl.BlockSpec(memory_space=pltpu.VMEM), pl.BlockSpec(memory_space=pltpu.HBM)
    return pl.pallas_call(
        masks_kernel,
        in_specs=[pl.BlockSpec(memory_space=pltpu.SMEM), vmem, hbm, hbm],
        out_specs=[vmem, vmem],
        out_shape=[
            jax.ShapeDtypeStruct((parts, depth), jnp.float32),
            jax.ShapeDtypeStruct((ab, depth), jnp.bfloat16),
        ],
        scratch_shapes=[
            pltpu.VMEM((amp_tiles.shape[0], depth), jnp.float32),
            pltpu.VMEM(int_tiles.shape, jnp.int32),
            pltpu.SemaphoreType.DMA((ab // PIECE + 1,)),
        ],
        compiler_params=pltpu.CompilerParams(vmem_limit_bytes=VMEM_LIMIT),
        cost_estimate=pl.CostEstimate(flops=ab * depth, bytes_accessed=4 * ab * depth, transcendentals=0),
    )(
        jnp.full((1,), first, jnp.int32),
        amp_tiles,
        pltpu.with_memory_space_constraint(int_tiles, pltpu.HBM),
        pltpu.with_memory_space_constraint(integrals, pltpu.HBM),
    )


def product_kernel(amps_ref, masked_ref, out_ref):
    for start in range(0, masked_ref.shape[0], BLOCK):
        block = slice(start, start + BLOCK)
        out_ref[:, block] = dot(amps_ref[...], masked_ref[block, :])


def product(amps, masked):
    rows, depth = amps.shape
    ab = masked.shape[0]
    vmem = pl.BlockSpec(memory_space=pltpu.VMEM)
    return pl.pallas_call(
        product_kernel,
        in_specs=[vmem, vmem],
        out_specs=vmem,
        out_shape=jax.ShapeDtypeStruct((rows, ab), jnp.float32),
        compiler_params=pltpu.CompilerParams(vmem_limit_bytes=VMEM_LIMIT),
        cost_estimate=pl.CostEstimate(
            flops=2 * rows * ab * depth, bytes_accessed=2 * (rows + ab) * depth + 4 * rows * ab, transcendentals=0
        ),
    )(amps, masked)


def sum_scatter(values, axis):
    sent = values.astype(jnp.float16)
    got = lax.all_to_all(sent, axis, 0, 0, tiled=True).astype(jnp.float32)
    return got.sum(0)


def on_device(amplitudes, amp_tiles, integrals, int_tiles, prior):
    f16, f32 = jnp.float16, jnp.float32
    local_rows, depth = amplitudes.shape
    ab = integrals.shape[0]
    own_rows = prior.shape[0]
    core, y = lax.axis_index("core"), lax.axis_index("y")
    n_x, n_zhi, n_core = lax.axis_size("x"), lax.axis_size("zhi"), lax.axis_size("core")

    zlo, n_zlo = lax.axis_index("zlo"), lax.axis_size("zlo")
    mask, masked = masks(y * local_rows // TILE, n_zlo, amp_tiles, int_tiles, integrals)
    def send(turn):
        pairs = [(2 * i + c, (i + (turn if c == 0 else n_zlo - turn)) % n_zlo * 2 + c) for i in range(n_zlo) for c in range(2)]
        return lax.ppermute(amplitudes, ("zlo", "core"), pairs)

    sent = [send(turn) for turn in range(1, n_zlo)]
    held = [amplitudes] + [jnp.where(core == 0, a, b) for a, b in zip(sent, sent[::-1])]
    near = []
    for source in range(n_zlo):
        block = held[0]
        for hop in range(1, n_zlo):
            block = jnp.where((zlo - hop) % n_zlo == source, held[hop], block)
        near.append(block)
    near = jnp.stack(near)
    near = (near.astype(f32) * mask[:, None, :]).astype(f16)
    amps = lax.all_gather(near, "y", axis=1, tiled=False)
    amps = amps.reshape(n_x, n_zhi, n_core, own_rows, depth)

    def product_of(c):
        rows = lax.dynamic_index_in_dim(amps, c, 2, False).astype(jnp.bfloat16)
        return product(rows.reshape(n_x * n_zhi * own_rows, depth), masked)

    crossing = lax.ppermute(product_of(1 - core), "core", [(0, 1), (1, 0)])
    mine = product_of(core)
    total = (mine + crossing) * (X_SCALE / AMP_SCALE)
    total = sum_scatter(total.reshape(n_x, n_zhi * own_rows, ab), "x") * (Z_SCALE / X_SCALE)
    total = sum_scatter(total.reshape(n_zhi, own_rows, ab), "zhi")
    return prior + total * (1 / Z_SCALE)


def solution(mesh):
    parts = Mesh(mesh.devices.reshape(SIZES), AXES)
    in_specs = (P(ROW, COL), P(None, COL), P(ROW, COL), P(ROW, COL), P(COL, ROW))
    return jax.shard_map(
        on_device, mesh=parts, in_specs=in_specs, out_specs=P(COL, ROW), check_vma=False
    )
```
